32 devices in a mesh: groups: 2 (over y), dp: 4 (over x, core), owner: 4 (over z).
Axes of the slice: x: 2, y: 2, z: 4, core: 2. Of those that a mesh axis runs over, the one named last changes fastest.
Arguments:
- acts: bfloat16 [8192, 6144], P(('groups', 'dp'), 'owner'), parts along dimension 0, may hold values from -45 to 45
- out_grads: bfloat16 [8192, 24576], P(('groups', 'dp'), 'owner'), parts along dimension 0, may hold values from -45 to 45
- weight_grad: bfloat16 [12288, 24576], P(('groups', 'owner'), 'dp'), parts along dimension 0, may hold values from -6 to 6
- old_bases: bfloat16 [8, 4, 16, 256, 256], P(('groups', 'owner'), 'dp'), parts along dimension 0, may hold values from -0.5 to 1.5
- owner_table: int32 [4, 30, 1], P('owner'), may hold values from 0 to 3; in each aligned block of 30 rows (0 to 29, 30 to 59, ..., all dimensions but the last counted through in order) at most 16 rows name the same one
Outputs:
- preconditioned: bfloat16 [12288, 24576], P(('groups', 'owner'), 'dp'), parts along dimension 0
- new_bases: bfloat16 [8, 4, 16, 256, 256], P(('groups', 'owner'), 'dp'), parts along dimension 0
- new_values: bfloat16 [8, 4, 16, 256], P(('groups', 'owner'), 'dp'), parts along dimension 0
The draws below stay inside these ranges and needn't reach their ends.
There are 2 independent parts, one for each index of `groups`. The reference program is written for one: setup_inputs(seed, part) draws one part's arguments, and reference() takes and returns one part's arrays. A program takes and returns all parts, laid end to end along the dimension named above; an argument that names none is the same for every part. Nothing has to cross between parts.
Inputs may be any that keep to these rules, and one draw needn't show every extreme that they name: `owner_table`: within one column's 30 entries a dp index appears at most 16 times; in some column one appears exactly 16 times; every dp index appears in some column.
All inputs are finite; a program needn't handle non-finite values.
Results may differ from the reference program's by a relative error of at most 0.039.
Values may be sent and summed in bfloat16 or wider, within the bound.
A program may use at most 192 MiB of HBM per device.

```python
import math
import jax
import jax.numpy as jnp
import numpy as np
from jax import lax

D = 6144
FF = 24576
BS = 256
ORTHO_STEPS = 8
TOK_DEV = 1024
TOKENS = 4096
NA = 6
NG = 24
NB = 30
CAP = 16
N_DP = 4
N_OWNER = 4


def shape_features(key, noise, low_col, high_col):
    rows, feats = noise.shape
    keys = jax.random.split(key, 5)
    region = jnp.arange(rows) * 64 // rows
    region_scale = jnp.exp(jax.random.uniform(keys[0], (64,), jnp.float32, math.log(0.4), math.log(2.5)))
    mixing = jax.random.uniform(keys[1], (64,), jnp.float32, 0.3, 1.0)
    token_scale = jnp.exp(jax.random.uniform(keys[2], (rows,), jnp.float32, -0.35, 0.35))
    column_scale = jnp.exp(jax.random.uniform(keys[3], (feats,), jnp.float32, math.log(low_col), math.log(high_col)))
    shared = jax.random.truncated_normal(keys[4], -4.0, 4.0, (rows, feats // 8), jnp.float32)
    grouped = jnp.repeat(shared, 8, axis=1)
    row_scale = (region_scale[region] * token_scale)[:, None]
    inner = column_scale[None, :] * noise + mixing[region][:, None] * grouped
    return row_scale * inner


def draw_acts(key, part):
    key = jax.random.fold_in(key, 11)
    first, second = jax.random.split(key)
    noise = jax.random.truncated_normal(first, -4.0, 4.0, (TOKENS, D), jnp.float32)
    return shape_features(second, noise, 0.5, 2.0).astype(jnp.bfloat16)


def draw_out_grads(key, part):
    key = jax.random.fold_in(key, 17)
    first, second = jax.random.split(key)
    noise = jax.random.truncated_normal(first, -4.0, 4.0, (TOKENS, FF), jnp.float32)
    return shape_features(second, noise, 0.5, 2.0).astype(jnp.bfloat16)


def draw_old_bases(key, part):
    key = jax.random.fold_in(key, 29)
    shape = (N_OWNER, N_DP, CAP, BS, BS)
    noise = jax.random.truncated_normal(key, -4.0, 4.0, shape, jnp.float32)
    identity = jnp.eye(BS, dtype=jnp.float32)
    return (identity + 0.35 / math.sqrt(BS) * noise).astype(jnp.bfloat16)


def block_levels(own_key, dims, cuts, least, high):
    level, own = 1.0, jax.random.fold_in(own_key, 6)
    for dim, parts in cuts:
        heights = jnp.exp(jax.random.uniform(jax.random.fold_in(own, dim), (parts,), jnp.float32, least / len(cuts), high / len(cuts)))
        level = level * jnp.repeat(heights, dims[dim] // parts).reshape([-1 if axis == dim else 1 for axis in range(len(dims))])
    return level


def deal_out(rng, own, number, rows, number_of, top, most, lean):
    sequence = jax.random.permutation(rng, number_of)
    packed, ordinary = shares(number_of, rows * top, most, lean, True), shares(number_of, rows * top, most, lean, False)
    places = jnp.arange(number_of)

    def named(lengths, turn):
        used = int((lengths > 0).sum())
        fixed = max(1, used // 4)
        moved = fixed + (places - fixed + turn * (used - fixed)) % max(1, number_of - fixed)
        return jnp.zeros((number_of,), jnp.int32).at[sequence[jnp.where(places < fixed, places, moved)]].set(jnp.asarray(lengths, jnp.int32))

    lengths = jnp.where(number % 4 == 0, named(packed, number // 4), named(ordinary, number - number // 4 - 1))
    mixed = jax.random.permutation(jax.random.fold_in(own, 3), number_of)
    giver, sink = mixed[0:number_of // 2 * 2:2], mixed[1:number_of // 2 * 2:2]
    margin = jnp.minimum(lengths[giver] - 1, most - lengths[sink]) // 2
    margin = jnp.where((giver == sequence[0]) | (sink == sequence[0]) | (lengths[sink] == 0), 0, jnp.maximum(margin, 0))
    moved = jax.random.randint(jax.random.fold_in(own, 4), (number_of // 2,), 0, 1 << 20) % (margin + 1)
    lengths = lengths.at[giver].add(-moved).at[sink].add(moved)
    labels = jnp.searchsorted(jnp.cumsum(lengths), jnp.arange(rows * top), side="right").astype(jnp.int32)
    table = labels.reshape(top, rows).T
    table = table[jax.random.permutation(jax.random.fold_in(own, 1), rows)]
    turn = jax.random.randint(jax.random.fold_in(own, 2), (rows, 1), 0, top)
    return jnp.take_along_axis(table, (jnp.arange(top)[None, :] + turn) % top, axis=1)


def shares(number_of, total, bound, slope, full):
    weights = [(1 << 20) // math.isqrt(rank ** slope) + 1 for rank in range(1, number_of + 1)]
    largest = bound if full else min(bound, max(-(-total // number_of), total * weights[0] // sum(weights)))
    least = 1 if total - largest >= number_of - 1 else 0
    counts, rest = [largest] + [least] * (number_of - 1), total - largest - least * (number_of - 1)
    while rest > 0:
        free = [i for i in range(1, number_of) if counts[i] < largest] or [i for i in range(1, number_of) if counts[i] < bound]
        mass, remaining = sum([weights[i] for i in free]), rest
        for i in free:
            more = min(bound - counts[i], max(1, remaining * weights[i] // mass), rest)
            counts[i] = counts[i] + more
            rest = rest - more
    return np.array(counts)


def normal_values(own_key, dims, deviation, bound, cuts=(), held_as=jnp.bfloat16):
    gain = block_levels(own_key, dims, cuts, -0.22, 0.18) if cuts else 1.0
    entries = jax.random.normal(own_key, dims, jnp.float32) * deviation * gain
    return jnp.minimum(jnp.maximum(entries, -bound), bound).astype(held_as)


def setup_inputs(seed: int = 0, part: int = 0) -> dict:
    key_list = jax.random.split(jax.random.key(seed), 6)
    part_splits = jax.random.split(jax.random.fold_in(key_list[5], part), 6)
    acts = draw_acts(jax.random.fold_in(jax.random.fold_in(key_list[5], part), 71), part)
    out_grads = draw_out_grads(jax.random.fold_in(jax.random.fold_in(key_list[5], part), 71), part)
    weight_grad = normal_values(part_splits[2], (D, FF), 1.0, 6.0, ((0, 4), (1, 4)))
    old_bases = draw_old_bases(jax.random.fold_in(jax.random.fold_in(key_list[5], part), 71), part)
    owner_table_keys = jax.random.split(jax.random.fold_in(key_list[4], 1), N_OWNER * NB // NB)
    owner_table_turns = jax.random.permutation(jax.random.fold_in(key_list[4], 3), N_OWNER * NB // NB)
    owner_table = jax.vmap(lambda own, number: deal_out(jax.random.fold_in(key_list[4], 2), own, number, NB, N_DP, 1, CAP, 1))(owner_table_keys, owner_table_turns).reshape((N_OWNER, NB, 1))
    return dict(acts=acts, out_grads=out_grads, weight_grad=weight_grad, old_bases=old_bases, owner_table=owner_table)


damping = 0.1
highest = lax.Precision.HIGHEST

def token_moments(values, blocks):
    shards = values.reshape(N_DP, TOK_DEV, blocks, BS)

    def accumulate(running, token_shard):
        widened = token_shard.astype(jnp.float32)
        shard_term = jnp.einsum('tai,taj->aij', widened, widened)
        shard_term = lax.optimization_barrier(shard_term.astype(jnp.bfloat16)).astype(jnp.float32)
        return (running + shard_term, None)
    running, unused = lax.scan(accumulate, jnp.zeros((blocks, BS, BS), jnp.float32), shards)
    return running / TOKENS

def refresh_blocks(moment, old_basis):
    rounded = lax.optimization_barrier(moment.astype(jnp.bfloat16)).astype(jnp.float32)
    product = jnp.einsum('sij,sjk->sik', rounded, old_basis.astype(jnp.float32), precision=highest)
    frobenius = jnp.sqrt(lax.optimization_barrier(jnp.sum(product * product, axis=(1, 2), keepdims=True)) + 1e-06)
    current = product / frobenius
    for counter in range(ORTHO_STEPS):
        gram_matrix = jnp.einsum('sji,sjk->sik', current, current, precision=highest)
        current = 1.5 * current - 0.5 * jnp.einsum('sij,sjk->sik', current, gram_matrix, precision=highest)
    applied = jnp.einsum('sij,sjk->sik', moment, current, precision=highest)
    values = lax.optimization_barrier(jnp.mean(applied * current, axis=1)) / (lax.optimization_barrier(jnp.mean(current * current, axis=1)) + 1e-06)
    return (current.astype(jnp.bfloat16), values.astype(jnp.bfloat16))

def reference(acts, out_grads, weight_grad, old_bases, owner_table):
    moment_a = token_moments(acts, D // BS).reshape(N_OWNER, NA, BS, BS)
    moment_g = token_moments(out_grads, FF // BS).reshape(N_OWNER, NG, BS, BS)
    moments = jnp.concatenate([moment_a, moment_g], axis=1)
    owners = owner_table[:, :, 0]
    block_order = jnp.arange(NB, dtype=jnp.int32)
    earlier = block_order[:, None] < block_order[None, :]
    same_owner = owners[:, :, None] == owners[:, None, :]
    slot_ranks = lax.optimization_barrier(jnp.sum(jnp.where(same_owner & earlier[None], 1, 0), axis=1)).astype(jnp.int32)
    columns = jnp.broadcast_to(jnp.arange(N_OWNER, dtype=jnp.int32)[:, None], (N_OWNER, NB))
    previous = old_bases[columns, owners, slot_ranks]
    refreshed, values = refresh_blocks(moments.reshape(N_OWNER * NB, BS, BS), previous.reshape(N_OWNER * NB, BS, BS))
    refreshed = refreshed.reshape(N_OWNER, NB, BS, BS)
    values = values.reshape(N_OWNER, NB, BS)
    new_bases = jnp.zeros((N_OWNER, N_DP, CAP, BS, BS), jnp.bfloat16).at[columns, owners, slot_ranks].set(refreshed)
    new_values = jnp.zeros((N_OWNER, N_DP, CAP, BS), jnp.bfloat16).at[columns, owners, slot_ranks].set(values)
    left_bases = refreshed[:, :NA].reshape(D // BS, BS, BS)
    left_values = values[:, :NA].reshape(D // BS, BS)
    right_basis = refreshed[:, NA:].reshape(FF // BS, BS, BS).astype(jnp.float32)
    right_values = values[:, NA:].reshape(FF // BS, BS).astype(jnp.float32)

    def precondition(inputs):
        grad_rows, left_block, scales = inputs
        left_block = left_block.astype(jnp.float32)
        widened = grad_rows.astype(jnp.float32).reshape(BS, FF // BS, BS)
        turned = jnp.einsum('ik,igj->kgj', left_block, widened)
        turned = lax.optimization_barrier(turned.astype(jnp.bfloat16)).astype(jnp.float32)
        rotated = jnp.einsum('kgj,gjl->kgl', turned, right_basis)
        divisor = scales.astype(jnp.float32)[:, None, None] * right_values[None, :, :] + damping
        scaled = lax.optimization_barrier((rotated / divisor).astype(jnp.bfloat16)).astype(jnp.float32)
        returned = jnp.einsum('kgl,gjl->kgj', scaled, right_basis)
        returned = lax.optimization_barrier(returned.astype(jnp.bfloat16)).astype(jnp.float32)
        return jnp.einsum('ik,kgj->igj', left_block, returned).astype(jnp.bfloat16).reshape(BS, FF)
    result = lax.map(precondition, (weight_grad.reshape(D // BS, BS, FF), left_bases, left_values))
    return (result.reshape(D, FF), new_bases, new_values)
```

```python
import functools

import jax
import jax.numpy as jnp
from jax import lax
from jax.experimental import pallas as pl
from jax.experimental.pallas import tpu as pltpu
from jax.sharding import PartitionSpec as P

BS = 256
ROWS = BS + 16
ORTHO_STEPS = 8
DAMPING = 0.1
F32 = jnp.float32
BF16 = jnp.bfloat16
MIB = 1 << 20


def dot(a, b, contract):
    return lax.dot_general(a, b, (contract, ((), ())), preferred_element_type=F32)


def ceil_div(a, b):
    return -(-a // b)


def moments_kernel(places_a, old_slot, held, acts_ref, grads_ref, old_ref, mom_ref, old_out_ref):
    step = pl.program_id(0)
    is_left = places_a[step] == 1

    @pl.when(is_left)
    def _():
        x = acts_ref[...]
        mom_ref[0] = dot(x, x, ((0,), (0,))).astype(BF16)

    @pl.when(jnp.logical_not(is_left))
    def _():
        x = grads_ref[...]
        mom_ref[0] = dot(x, x, ((0,), (0,))).astype(BF16)

    old_out_ref[0] = jnp.where(held[step] == 1, old_ref[0], jnp.zeros_like(old_ref[0]))


def moments(acts, grads, old, is_left, block_a, block_g, old_slot, held):
    tokens = acts.shape[0]
    count = is_left.shape[0]

    def kernel(is_left, block_a, block_g, old_slot, held, *refs):
        moments_kernel(is_left, old_slot, held, *refs)

    return pl.pallas_call(
        kernel,
        grid_spec=pltpu.PrefetchScalarGridSpec(
            num_scalar_prefetch=5,
            grid=(count,),
            in_specs=[
                pl.BlockSpec((tokens, BS), lambda i, l, a, g, s, h: (0, a[i])),
                pl.BlockSpec((tokens, BS), lambda i, l, a, g, s, h: (0, g[i])),
                pl.BlockSpec((1, BS, BS), lambda i, l, a, g, s, h: (s[i], 0, 0)),
            ],
            out_specs=[
                pl.BlockSpec((1, BS, BS), lambda i, l, a, g, s, h: (i, 0, 0)),
                pl.BlockSpec((1, BS, BS), lambda i, l, a, g, s, h: (i, 0, 0)),
            ],
        ),
        out_shape=[jax.ShapeDtypeStruct((count, BS, BS), BF16)] * 2,
        compiler_params=pltpu.CompilerParams(vmem_limit_bytes=32 * MIB),
        cost_estimate=pl.CostEstimate(
            flops=2 * count * tokens * BS * BS, bytes_accessed=24 * MIB, transcendentals=0
        ),
        name="moments",
    )(is_left, block_a, block_g, old_slot, held, acts, grads, old)


def reduce_kernel(n, slots, mom, old, mom_out, old_out, near, far, own, near_send, near_recv, far_send, far_recv):
    me = lax.axis_index("dp")
    pairs = n // 2
    chip, core = me // 2, lax.rem(me, 2)
    partner = chip * 2 + (1 - core)

    barrier = pltpu.get_barrier_semaphore()
    pl.semaphore_signal(barrier, inc=1, device_id={"dp": partner})
    for k in range(1, pairs):
        there = lax.rem(chip + k, pairs) * 2 + core
        pl.semaphore_signal(barrier, inc=1, device_id={"dp": there})
    pl.semaphore_wait(barrier, pairs)

    def to_partner(k, part):
        target = lax.rem(chip + k, pairs) * 2 + (1 - core)
        return pltpu.make_async_remote_copy(
            src_ref=(old, mom)[part].at[target],
            dst_ref=near.at[k - 1, part],
            send_sem=near_send.at[k - 1, part],
            recv_sem=near_recv.at[k - 1, part],
            device_id={"dp": partner},
        )

    def to_chip(k, part):
        return pltpu.make_async_remote_copy(
            src_ref=own.at[k - 1, part],
            dst_ref=far.at[k - 1, part],
            send_sem=far_send.at[k - 1, part],
            recv_sem=far_recv.at[k - 1, part],
            device_id={"dp": lax.rem(chip + k, pairs) * 2 + core},
        )

    order = [(k, part) for part in (0, 1) for k in range(1, pairs + 1)]
    for k, part in order:
        to_partner(k, part).start()
    for k, part in order:
        to_partner(k, part).wait()
        source = (old, mom)[part]
        mine = lax.rem(chip + k, pairs) * 2 + core

        @pl.loop(0, slots)
        def _(s):
            own[k - 1, part, s] = (
                source[mine, s].astype(F32) + near[k - 1, part, s].astype(F32)
            ).astype(BF16)

        if k < pairs:
            to_chip(k, part).start()
    for part in (0, 1):
        for k in range(1, pairs):
            to_chip(k, part).wait()

        @pl.loop(0, slots)
        def _(s):
            total = own[pairs - 1, part, s].astype(F32)
            for k in range(1, pairs):
                total = total + far[k - 1, part, s].astype(F32)
            if part == 0:
                old_out[s] = total.astype(BF16)
            else:
                mom_out[s] = total


def reduce_blocks(n, slots, mom, old):
    pairs = n // 2
    vmem = pl.BlockSpec(memory_space=pltpu.VMEM)
    buffer = pltpu.VMEM((pairs, 2, slots, BS, BS), BF16)
    return pl.pallas_call(
        functools.partial(reduce_kernel, n, slots),
        out_shape=[
            jax.ShapeDtypeStruct((slots, BS, BS), F32),
            jax.ShapeDtypeStruct((slots, BS, BS), BF16),
        ],
        in_specs=[vmem, vmem],
        out_specs=[vmem, vmem],
        scratch_shapes=[buffer] * 3 + [pltpu.SemaphoreType.DMA((pairs, 2))] * 4,
        compiler_params=pltpu.CompilerParams(
            collective_id=0, has_side_effects=True, vmem_limit_bytes=56 * MIB
        ),
        cost_estimate=pl.CostEstimate(flops=10 * MIB, bytes_accessed=16 * MIB, transcendentals=0),
        name="reduce_blocks",
    )(mom, old)


def refresh_kernel(group, tokens, mom_ref, old_ref, out_ref, current):
    for s in range(group):
        moment = mom_ref[s] * (1.0 / tokens)
        product = dot(moment.astype(BF16), old_ref[s], ((1,), (0,)))
        current[s] = product / jnp.sqrt(jnp.sum(product * product) + 1e-06)

    @pl.loop(0, ORTHO_STEPS)
    def _(step):
        rounded = [current[s].astype(BF16) for s in range(group)]
        grams = [dot(y, y, ((0,), (0,))).astype(BF16) for y in rounded]
        for s in range(group):
            current[s] = 1.5 * current[s] - 0.5 * dot(rounded[s], grams[s], ((1,), (0,)))

    for s in range(group):
        moment = mom_ref[s] * (1.0 / tokens)
        high = moment.astype(BF16)
        low = (moment - high.astype(F32)).astype(BF16)
        y = current[s]
        basis = y.astype(BF16)
        applied = dot(high, basis, ((1,), (0,))) + dot(low, basis, ((1,), (0,)))
        top = jnp.mean(applied * y, axis=0, keepdims=True)
        value = top / (jnp.mean(y * y, axis=0, keepdims=True) + 1e-06)
        out_ref[s, 0:BS] = basis
        out_ref[s, BS:ROWS] = jnp.broadcast_to(value, (ROWS - BS, BS)).astype(BF16)


def refresh(mom, old, tokens):
    slots = mom.shape[0]
    group = 4 if slots % 4 == 0 else (2 if slots % 2 == 0 else 1)
    block = pl.BlockSpec((group, BS, BS), lambda i: (i, 0, 0))
    return pl.pallas_call(
        functools.partial(refresh_kernel, group, tokens),
        grid=(slots // group,),
        in_specs=[block, block],
        out_specs=pl.BlockSpec((group, ROWS, BS), lambda i: (i, 0, 0)),
        out_shape=jax.ShapeDtypeStruct((slots, ROWS, BS), BF16),
        scratch_shapes=[pltpu.VMEM((group, BS, BS), F32)],
        compiler_params=pltpu.CompilerParams(vmem_limit_bytes=32 * MIB),
        cost_estimate=pl.CostEstimate(
            flops=36 * slots * BS**3, bytes_accessed=8 * MIB, transcendentals=0
        ),
        name="refresh",
    )(mom, old)


def spread_kernel(
    n, columns, left, fresh, column_blocks, right, held, up_send, up_recv, down_send, down_recv,
    give_send, give_recv, all_send, all_recv, local_sem,
):
    me, here = lax.axis_index("dp"), lax.axis_index("owner")
    per = n // columns
    above = jnp.minimum(here + 1, columns - 1)
    below = jnp.maximum(here - 1, 0)
    has_above, has_below = here < columns - 1, here > 0

    barrier = pltpu.get_barrier_semaphore()
    for k in range(1, n):
        pl.semaphore_signal(barrier, inc=1, device_id={"dp": lax.rem(me + k, n)})

    @pl.when(has_above)
    def _():
        pl.semaphore_signal(barrier, inc=1, device_id={"owner": above})

    @pl.when(has_below)
    def _():
        pl.semaphore_signal(barrier, inc=1, device_id={"owner": below})

    pl.semaphore_wait(barrier, n - 1 + jnp.where(has_above, 1, 0) + jnp.where(has_below, 1, 0))

    held[here] = fresh[left:]

    def along(k, column, send, recv, there):
        return pltpu.make_async_remote_copy(
            src_ref=held.at[column],
            dst_ref=held.at[column],
            send_sem=send.at[k],
            recv_sem=recv.at[k],
            device_id={"owner": there},
        )

    def clamp(column):
        return jnp.clip(column, 0, columns - 1)

    def up(k, column):
        return along(k, clamp(column), up_send, up_recv, above)

    def down(k, column):
        return along(k, clamp(column), down_send, down_recv, below)

    def give(column, target):
        return pltpu.make_async_remote_copy(
            src_ref=held.at[column],
            dst_ref=right.at[me],
            send_sem=give_send.at[target],
            recv_sem=give_recv.at[me],
            device_id={"dp": target},
        )

    def taken(source):
        return pltpu.make_async_remote_copy(
            src_ref=held.at[0],
            dst_ref=right.at[source],
            send_sem=give_send.at[source],
            recv_sem=give_recv.at[source],
            device_id={"dp": source},
        )

    def keep(column):
        return pltpu.make_async_copy(held.at[column], right.at[me], local_sem.at[0])

    def share(column):
        for h in range(per):
            target = column * per + h

            @pl.when(target != me)
            def _():
                give(column, target).start()

            @pl.when(target == me)
            def _():
                keep(column).start()

    def to_all(k):
        return pltpu.make_async_remote_copy(
            src_ref=fresh,
            dst_ref=column_blocks.at[me],
            send_sem=all_send.at[k - 1],
            recv_sem=all_recv.at[k - 1],
            device_id={"dp": lax.rem(me + k, n)},
        )

    def from_all(k):
        return pltpu.make_async_remote_copy(
            src_ref=fresh,
            dst_ref=column_blocks.at[lax.rem(me + n - k, n)],
            send_sem=all_send.at[k - 1],
            recv_sem=all_recv.at[k - 1],
            device_id={"dp": lax.rem(me + k, n)},
        )

    mine = pltpu.make_async_copy(fresh, column_blocks.at[me], local_sem.at[1])
    for k in range(columns - 1):
        sends_up = has_above & (here - k >= 0)
        sends_down = has_below & (here + k <= columns - 1)

        @pl.when(sends_up)
        def _():
            up(k, here - k).start()

        @pl.when(sends_down)
        def _():
            down(k, here + k).start()

        if k == 0:
            share(here)
            mine.start()
            for j in range(1, n):
                to_all(j).start()

        @pl.when(here - 1 - k >= 0)
        def _():
            up(k, here - 1 - k).wait_recv()
            share(clamp(here - 1 - k))

        @pl.when(here + 1 + k <= columns - 1)
        def _():
            down(k, here + 1 + k).wait_recv()
            share(clamp(here + 1 + k))

    for k in range(columns - 1):

        @pl.when(has_above & (here - k >= 0))
        def _():
            up(k, here - k).wait_send()

        @pl.when(has_below & (here + k <= columns - 1))
        def _():
            down(k, here + k).wait_send()

    mine.wait()
    keep(here).wait()
    for k in range(1, n):
        to_all(k).wait_send()
        from_all(k).wait_recv()
        other = lax.rem(me + k, n)
        taken(other).wait_send()
        taken(other).wait_recv()


def spread(n, columns, left, fresh):
    slots = fresh.shape[0]
    dma = pltpu.SemaphoreType.DMA
    vmem = pl.BlockSpec(memory_space=pltpu.VMEM)
    return pl.pallas_call(
        functools.partial(spread_kernel, n, columns, left),
        out_shape=[
            jax.ShapeDtypeStruct((n, slots, ROWS, BS), BF16),
            jax.ShapeDtypeStruct((n, slots - left, ROWS, BS), BF16),
        ],
        in_specs=[vmem],
        out_specs=[vmem, vmem],
        scratch_shapes=[pltpu.VMEM((columns, slots - left, ROWS, BS), BF16)]
        + [dma((columns - 1,))] * 4
        + [dma((n,))] * 2
        + [dma((n - 1,))] * 2
        + [dma((2,))],
        compiler_params=pltpu.CompilerParams(
            collective_id=1, has_side_effects=True, vmem_limit_bytes=56 * MIB
        ),
        cost_estimate=pl.CostEstimate(flops=0, bytes_accessed=16 * MIB, transcendentals=0),
        name="spread",
    )(fresh)


def precondition_kernel(
    chunk, place, used, grad_ref, left_ref, la_ref, right_ref, block_ref, out_ref, bases_ref, turned_left
):
    row, part = pl.program_id(0), pl.program_id(1)
    slot = jnp.minimum(row * pl.num_programs(1) + part, used.shape[0] - 1)

    @pl.when(part == 0)
    def _():
        turned_left[...] = left_ref[0, 0:BS].T

    left = left_ref[0, 0:BS]
    la = la_ref[0][:, 0:1]
    for j in range(chunk):
        cols = slice(j * BS, (j + 1) * BS)
        g = part * chunk + j
        basis = right_ref[g, 0:BS]
        lg = right_ref[g, BS : BS + 16].astype(F32)[0:1]
        turned = dot(turned_left[...], grad_ref[:, cols], ((1,), (0,))).astype(BF16)
        rotated = dot(turned, basis, ((1,), (0,)))
        scaled = (rotated / (la * lg + DAMPING)).astype(BF16)
        returned = dot(scaled, basis, ((1,), (1,))).astype(BF16)
        out_ref[:, cols] = dot(left, returned, ((1,), (0,))).astype(BF16)
    block = block_ref[0, 0:BS]
    bases_ref[0] = jnp.where(used[slot] == 1, block, jnp.zeros_like(block))


def precondition(grad, blocks, left_index, la, right, place, used):
    rows, width = grad.shape[0] // BS, grad.shape[1] // BS
    cap = place.shape[0]
    chunk = next(c for c in (6, 4, 3, 2, 1) if width % c == 0 and rows * (width // c) >= cap)
    parts = width // chunk

    def slot(r, p):
        return jnp.minimum(r * parts + p, cap - 1)

    return pl.pallas_call(
        functools.partial(precondition_kernel, chunk),
        grid_spec=pltpu.PrefetchScalarGridSpec(
            num_scalar_prefetch=2,
            grid=(rows, parts),
            in_specs=[
                pl.BlockSpec((BS, chunk * BS), lambda r, p, at, u: (r, p)),
                pl.BlockSpec((1, ROWS, BS), lambda r, p, at, u: (left_index(r), 0, 0)),
                pl.BlockSpec((1, BS, 128), lambda r, p, at, u: (r, 0, 0)),
                pl.BlockSpec(right.shape, lambda r, p, at, u: (0, 0, 0)),
                pl.BlockSpec((1, ROWS, BS), lambda r, p, at, u: (at[slot(r, p)], 0, 0)),
            ],
            out_specs=[
                pl.BlockSpec((BS, chunk * BS), lambda r, p, at, u: (r, p)),
                pl.BlockSpec((1, BS, BS), lambda r, p, at, u: (slot(r, p), 0, 0)),
            ],
            scratch_shapes=[pltpu.VMEM((BS, BS), BF16)],
        ),
        out_shape=[
            jax.ShapeDtypeStruct(grad.shape, BF16),
            jax.ShapeDtypeStruct((cap, BS, BS), BF16),
        ],
        compiler_params=pltpu.CompilerParams(vmem_limit_bytes=48 * MIB),
        cost_estimate=pl.CostEstimate(
            flops=8 * BS**3 * rows * width, bytes_accessed=44 * MIB, transcendentals=0
        ),
        name="precondition",
    )(place, used, grad, blocks, la, right, blocks)


def shards(acts, out_grads, weight_grad, old_bases, owner_table):
    n, columns = lax.axis_size("dp"), lax.axis_size("owner")
    me = lax.axis_index("dp")
    blocks_a, blocks_g = acts.shape[1] // BS, out_grads.shape[1] // BS
    count = blocks_a + blocks_g
    cap = old_bases.shape[2]
    tokens = acts.shape[0] * n
    left, right = ceil_div(blocks_a, n), ceil_div(blocks_g, n)
    slots = left + right

    owners = owner_table[0, :, 0]
    order = jnp.arange(count, dtype=jnp.int32)
    same = owners[:, None] == owners[None, :]
    ranks = jnp.sum(jnp.where(same & (order[:, None] < order[None, :]), 1, 0), axis=0).astype(jnp.int32)

    is_left, block_a, block_g, block, real = [], [], [], [], []
    last_a, last_g = 0, 0
    for r in range(n):
        for s in range(slots):
            if s < left:
                b = r * left + s
                real.append(int(b < blocks_a))
                last_a = min(b, blocks_a - 1)
                is_left.append(1)
                block.append(last_a)
            else:
                b = r * right + s - left
                real.append(int(b < blocks_g))
                last_g = min(b, blocks_g - 1)
                is_left.append(0)
                block.append(blocks_a + last_g)
            block_a.append(last_a)
            block_g.append(last_g)
    as_int = functools.partial(jnp.array, dtype=jnp.int32)
    block_at = as_int(block)
    held = (jnp.take(owners, block_at) == me) & (as_int(real) == 1)
    old_slot = jnp.where(held, jnp.take(ranks, block_at), 0).astype(jnp.int32)

    mom, old = moments(
        acts, out_grads, old_bases[0, 0],
        as_int(is_left), as_int(block_a), as_int(block_g), old_slot, held.astype(jnp.int32),
    )
    shape = (n, slots, BS, BS)
    mom, old = reduce_blocks(n, slots, mom.reshape(shape), old.reshape(shape))
    fresh = refresh(mom, old, tokens)
    blocks, rights = spread(n, columns, left, fresh)
    blocks = blocks.reshape(n * slots, ROWS, BS)

    width = weight_grad.shape[1] // BS
    rights = rights.reshape(n * right, ROWS, BS)
    if n * right != width:
        rights = lax.dynamic_slice_in_dim(rights, me % (n // columns) * width, width, 0)

    def left_index(a):
        return a // left * slots + a % left

    values = blocks[:, BS]
    left_at = [left_index(a) for a in range(blocks_a)]
    la = jnp.concatenate([values[i : i + 1] for i in left_at]).astype(F32)
    la = jnp.broadcast_to(la[:, :, None], (blocks_a, BS, 128))

    places = as_int([left_index(a) for a in range(blocks_a)]
                    + [g // right * slots + left + g % right for g in range(blocks_g)])
    hit = (owners[None, :] == me) & (ranks[None, :] == jnp.arange(cap, dtype=jnp.int32)[:, None])
    place = jnp.sum(jnp.where(hit, places[None, :], 0), axis=1).astype(jnp.int32)
    used = jnp.any(hit, axis=1)
    chosen = (place[:, None] == jnp.arange(n * slots, dtype=jnp.int32)[None, :]) & used[:, None]
    new_values = jnp.dot(chosen.astype(BF16), values, preferred_element_type=F32).astype(BF16)

    result, new_bases = precondition(
        weight_grad, blocks, left_index, la, rights, place, used.astype(jnp.int32)
    )
    return (result, new_bases[None, None], new_values[None, None])


def solution(mesh):
    placed = (
        P(("groups", "dp"), "owner"),
        P(("groups", "dp"), "owner"),
        P(("groups", "owner"), "dp"),
        P(("groups", "owner"), "dp", None, None, None),
        P("owner", None, None),
    )
    return jax.shard_map(
        shards,
        mesh=mesh,
        in_specs=placed,
        out_specs=(
            P(("groups", "owner"), "dp"),
            P(("groups", "owner"), "dp", None, None, None),
            P(("groups", "owner"), "dp", None, None),
        ),
        check_vma=False,
    )
```

```python
import functools

import jax
import jax.numpy as jnp
from jax import lax
from jax.experimental import pallas as pl
from jax.experimental.pallas import tpu as pltpu
from jax.sharding import PartitionSpec as P

BS = 256
ROWS = BS + 16
ORTHO_STEPS = 8
DAMPING = 0.1
F32 = jnp.float32
BF16 = jnp.bfloat16
MIB = 1 << 20


def dot(a, b, contract):
    return lax.dot_general(a, b, (contract, ((), ())), preferred_element_type=F32)


def ceil_div(a, b):
    return -(-a // b)


def moments_kernel(left, right, acts_ref, grads_ref, out_ref):
    for s in range(left + right):
        ref, at = (acts_ref, s) if s < left else (grads_ref, s - left)
        x = ref[:, at * BS : (at + 1) * BS]
        out_ref[0, s] = dot(x, x, ((0,), (0,))).astype(BF16)


def moments(n, left, right, acts, grads):
    tokens = acts.shape[0]
    slots = left + right
    last_a = acts.shape[1] // (left * BS) - 1
    last_g = grads.shape[1] // (right * BS) - 1
    return pl.pallas_call(
        functools.partial(moments_kernel, left, right),
        grid=(n,),
        in_specs=[
            pl.BlockSpec((tokens, left * BS), lambda r: (0, jnp.minimum(r, last_a))),
            pl.BlockSpec((tokens, right * BS), lambda r: (0, jnp.minimum(r, last_g))),
        ],
        out_specs=pl.BlockSpec((1, slots, BS, BS), lambda r: (r, 0, 0, 0)),
        out_shape=jax.ShapeDtypeStruct((n, slots, BS, BS), BF16),
        compiler_params=pltpu.CompilerParams(vmem_limit_bytes=40 * MIB),
        cost_estimate=pl.CostEstimate(
            flops=2 * n * slots * tokens * BS * BS, bytes_accessed=20 * MIB, transcendentals=0
        ),
        name="moments",
    )(acts, grads)


def reduce_kernel(n, slots, mom, out, near, far, own, near_send, near_recv, far_send, far_recv):
    me = lax.axis_index("dp")
    pairs = n // 2
    chip, core = me // 2, lax.rem(me, 2)
    partner = chip * 2 + (1 - core)
    half = slots // 2
    pieces = [(0, half), (half, slots)]

    barrier = pltpu.get_barrier_semaphore()
    pl.semaphore_signal(barrier, inc=1, device_id={"dp": partner})
    for k in range(1, pairs):
        there = lax.rem(chip + k, pairs) * 2 + core
        pl.semaphore_signal(barrier, inc=1, device_id={"dp": there})
    pl.semaphore_wait(barrier, pairs)

    def to_partner(k, part):
        target = lax.rem(chip + k, pairs) * 2 + (1 - core)
        some = pl.ds(pieces[part][0], pieces[part][1] - pieces[part][0])
        return pltpu.make_async_remote_copy(
            src_ref=mom.at[target, some],
            dst_ref=near.at[k - 1, some],
            send_sem=near_send.at[k - 1, part],
            recv_sem=near_recv.at[k - 1, part],
            device_id={"dp": partner},
        )

    def to_chip(k, part):
        some = pl.ds(pieces[part][0], pieces[part][1] - pieces[part][0])
        return pltpu.make_async_remote_copy(
            src_ref=own.at[k - 1, some],
            dst_ref=far.at[k - 1, some],
            send_sem=far_send.at[k - 1, part],
            recv_sem=far_recv.at[k - 1, part],
            device_id={"dp": lax.rem(chip + k, pairs) * 2 + core},
        )

    order = [(k, part) for k in range(1, pairs + 1) for part in (0, 1)]
    for k, part in order:
        to_partner(k, part).start()
    for k, part in order:
        to_partner(k, part).wait()
        mine = lax.rem(chip + k, pairs) * 2 + core

        @pl.loop(*pieces[part])
        def _(s):
            own[k - 1, s] = (mom[mine, s].astype(F32) + near[k - 1, s].astype(F32)).astype(BF16)

        if k < pairs:
            to_chip(k, part).start()
    for part in (0, 1):
        for k in range(1, pairs):
            to_chip(k, part).wait()

        @pl.loop(*pieces[part])
        def _(s):
            total = own[pairs - 1, s].astype(F32)
            for k in range(1, pairs):
                total = total + far[k - 1, s].astype(F32)
            out[s] = total


def reduce_blocks(n, slots, mom):
    pairs = n // 2
    vmem = pl.BlockSpec(memory_space=pltpu.VMEM)
    buffer = pltpu.VMEM((pairs, slots, BS, BS), BF16)
    return pl.pallas_call(
        functools.partial(reduce_kernel, n, slots),
        out_shape=jax.ShapeDtypeStruct((slots, BS, BS), F32),
        in_specs=[vmem],
        out_specs=vmem,
        scratch_shapes=[buffer] * 3 + [pltpu.SemaphoreType.DMA((pairs, 2))] * 4,
        compiler_params=pltpu.CompilerParams(
            collective_id=0, has_side_effects=True, vmem_limit_bytes=40 * MIB
        ),
        cost_estimate=pl.CostEstimate(flops=10 * MIB, bytes_accessed=16 * MIB, transcendentals=0),
        name="reduce_blocks",
    )(mom)


def refresh_kernel(group, tokens, at, mom_ref, *refs):
    old_refs, (out_ref, current) = refs[:group], refs[group:]
    for s in range(group):
        moment = mom_ref[s] * (1.0 / tokens)
        product = dot(moment.astype(BF16), old_refs[s][0], ((1,), (0,)))
        current[s] = product / jnp.sqrt(jnp.sum(product * product) + 1e-06)

    @pl.loop(0, ORTHO_STEPS)
    def _(step):
        rounded = [current[s].astype(BF16) for s in range(group)]
        grams = [dot(y, y, ((0,), (0,))).astype(BF16) for y in rounded]
        for s in range(group):
            current[s] = 1.5 * current[s] - 0.5 * dot(rounded[s], grams[s], ((1,), (0,)))

    for s in range(group):
        moment = mom_ref[s] * (1.0 / tokens)
        high = moment.astype(BF16)
        low = (moment - high.astype(F32)).astype(BF16)
        y = current[s]
        basis = y.astype(BF16)
        applied = dot(high, basis, ((1,), (0,))) + dot(low, basis, ((1,), (0,)))
        top = jnp.mean(applied * y, axis=0, keepdims=True)
        value = top / (jnp.mean(y * y, axis=0, keepdims=True) + 1e-06)
        out_ref[s, 0:BS] = basis
        out_ref[s, BS:ROWS] = jnp.broadcast_to(value, (ROWS - BS, BS)).astype(BF16)


def refresh(mom, old, at, tokens):
    slots = mom.shape[0]
    group = 4 if slots % 4 == 0 else (2 if slots % 2 == 0 else 1)

    def previous(j):
        return pl.BlockSpec((1, BS, BS), lambda i, at: (at[i * group + j], 0, 0))

    return pl.pallas_call(
        functools.partial(refresh_kernel, group, tokens),
        grid_spec=pltpu.PrefetchScalarGridSpec(
            num_scalar_prefetch=1,
            grid=(slots // group,),
            in_specs=[pl.BlockSpec((group, BS, BS), lambda i, at: (i, 0, 0))]
            + [previous(j) for j in range(group)],
            out_specs=pl.BlockSpec((group, ROWS, BS), lambda i, at: (i, 0, 0)),
            scratch_shapes=[pltpu.VMEM((group, BS, BS), F32)],
        ),
        out_shape=jax.ShapeDtypeStruct((slots, ROWS, BS), BF16),
        compiler_params=pltpu.CompilerParams(vmem_limit_bytes=32 * MIB),
        cost_estimate=pl.CostEstimate(
            flops=36 * slots * BS**3, bytes_accessed=8 * MIB, transcendentals=0
        ),
        name="refresh",
    )(at, mom, *([old] * group))


def spread_kernel(
    n, columns, left, fresh, column_blocks, right, held, up_send, up_recv, down_send, down_recv,
    give_send, give_recv, chip_send, chip_recv, core_send, core_recv, local_sem,
):
    me, here = lax.axis_index("dp"), lax.axis_index("owner")
    per = n // columns
    above = jnp.minimum(here + 1, columns - 1)
    below = jnp.maximum(here - 1, 0)
    has_above, has_below = here < columns - 1, here > 0

    barrier = pltpu.get_barrier_semaphore()
    for k in range(1, n):
        pl.semaphore_signal(barrier, inc=1, device_id={"dp": lax.rem(me + k, n)})

    @pl.when(has_above)
    def _():
        pl.semaphore_signal(barrier, inc=1, device_id={"owner": above})

    @pl.when(has_below)
    def _():
        pl.semaphore_signal(barrier, inc=1, device_id={"owner": below})

    pl.semaphore_wait(barrier, n - 1 + jnp.where(has_above, 1, 0) + jnp.where(has_below, 1, 0))

    held[here] = fresh[left:]

    def along(k, column, send, recv, there):
        return pltpu.make_async_remote_copy(
            src_ref=held.at[column],
            dst_ref=held.at[column],
            send_sem=send.at[k],
            recv_sem=recv.at[k],
            device_id={"owner": there},
        )

    def clamp(column):
        return jnp.clip(column, 0, columns - 1)

    def up(k, column):
        return along(k, clamp(column), up_send, up_recv, above)

    def down(k, column):
        return along(k, clamp(column), down_send, down_recv, below)

    def give(column, target):
        return pltpu.make_async_remote_copy(
            src_ref=held.at[column],
            dst_ref=right.at[me],
            send_sem=give_send.at[target],
            recv_sem=give_recv.at[me],
            device_id={"dp": target},
        )

    def taken(source):
        return pltpu.make_async_remote_copy(
            src_ref=held.at[0],
            dst_ref=right.at[source],
            send_sem=give_send.at[source],
            recv_sem=give_recv.at[source],
            device_id={"dp": source},
        )

    def keep(column):
        return pltpu.make_async_copy(held.at[column], right.at[me], local_sem.at[0])

    def share(column):
        for h in range(per):
            target = column * per + h

            @pl.when(target != me)
            def _():
                give(column, target).start()

            @pl.when(target == me)
            def _():
                keep(column).start()

    pairs = n // 2
    chip, core = me // 2, lax.rem(me, 2)
    partner = chip * 2 + (1 - core)

    def to_chip(k):
        return pltpu.make_async_remote_copy(
            src_ref=fresh,
            dst_ref=column_blocks.at[me],
            send_sem=chip_send.at[k - 1],
            recv_sem=chip_recv.at[k - 1],
            device_id={"dp": lax.rem(chip + k, pairs) * 2 + core},
        )

    def source(k):
        return lax.rem(chip + pairs - k, pairs) * 2 + core

    def to_partner(k):
        return pltpu.make_async_remote_copy(
            src_ref=fresh if k == 0 else column_blocks.at[source(k)],
            dst_ref=column_blocks.at[source(k)],
            send_sem=core_send.at[k],
            recv_sem=core_recv.at[k],
            device_id={"dp": partner},
        )

    mine = pltpu.make_async_copy(fresh, column_blocks.at[me], local_sem.at[1])
    for k in range(columns - 1):
        sends_up = has_above & (here - k >= 0)
        sends_down = has_below & (here + k <= columns - 1)

        @pl.when(sends_up)
        def _():
            up(k, here - k).start()

        @pl.when(sends_down)
        def _():
            down(k, here + k).start()

        if k == 0:
            share(here)
            mine.start()
            for j in range(1, pairs):
                to_chip(j).start()
            to_partner(0).start()

        if k == 1:
            for j in range(1, pairs):
                to_chip(j).wait_recv()
                to_partner(j).start()

        @pl.when(here - 1 - k >= 0)
        def _():
            up(k, here - 1 - k).wait_recv()
            share(clamp(here - 1 - k))

        @pl.when(here + 1 + k <= columns - 1)
        def _():
            down(k, here + 1 + k).wait_recv()
            share(clamp(here + 1 + k))

    for k in range(columns - 1):

        @pl.when(has_above & (here - k >= 0))
        def _():
            up(k, here - k).wait_send()

        @pl.when(has_below & (here + k <= columns - 1))
        def _():
            down(k, here + k).wait_send()

    mine.wait()
    keep(here).wait()
    for k in range(pairs):
        to_partner(k).wait()
        if k > 0:
            to_chip(k).wait_send()
    for k in range(1, n):
        other = lax.rem(me + k, n)
        taken(other).wait_send()
        taken(other).wait_recv()


def spread(n, columns, left, fresh):
    slots = fresh.shape[0]
    dma = pltpu.SemaphoreType.DMA
    vmem = pl.BlockSpec(memory_space=pltpu.VMEM)
    return pl.pallas_call(
        functools.partial(spread_kernel, n, columns, left),
        out_shape=[
            jax.ShapeDtypeStruct((n, slots, ROWS, BS), BF16),
            jax.ShapeDtypeStruct((n, slots - left, ROWS, BS), BF16),
        ],
        in_specs=[vmem],
        out_specs=[vmem, vmem],
        scratch_shapes=[pltpu.VMEM((columns, slots - left, ROWS, BS), BF16)]
        + [dma((columns - 1,))] * 4
        + [dma((n,))] * 2
        + [dma((max(1, n // 2 - 1),))] * 2
        + [dma((n // 2,))] * 2
        + [dma((2,))],
        compiler_params=pltpu.CompilerParams(
            collective_id=1, has_side_effects=True, vmem_limit_bytes=56 * MIB
        ),
        cost_estimate=pl.CostEstimate(flops=0, bytes_accessed=16 * MIB, transcendentals=0),
        name="spread",
    )(fresh)


def precondition_kernel(
    rows, place, used, grad_ref, left_ref, turned_left_ref, la_ref, right_ref, block_ref, out_ref, bases_ref,
):
    slot = jnp.minimum(pl.program_id(0), used.shape[0] - 1)
    basis = right_ref[0, 0:BS]
    lg = right_ref[0, BS:ROWS].astype(F32)[0:1]
    turned = [
        dot(turned_left_ref[a], grad_ref[a * BS : (a + 1) * BS], ((1,), (0,))).astype(BF16)
        for a in range(rows)
    ]
    rotated = [dot(turned[a], basis, ((1,), (0,))) for a in range(rows)]
    scaled = [
        (rotated[a] / (la_ref[a][:, 0:1] * lg + DAMPING)).astype(BF16) for a in range(rows)
    ]
    returned = [dot(scaled[a], basis, ((1,), (1,))).astype(BF16) for a in range(rows)]
    for a in range(rows):
        out_ref[a * BS : (a + 1) * BS] = dot(left_ref[a], returned[a], ((1,), (0,))).astype(BF16)
    block = block_ref[0, 0:BS]
    bases_ref[0] = jnp.where(used[slot] == 1, block, jnp.zeros_like(block))


def precondition(grad, left, turned_left, la, right, blocks, place, used):
    rows, width = grad.shape[0] // BS, grad.shape[1] // BS
    cap = place.shape[0]
    assert width >= cap

    def slot(g):
        return jnp.minimum(g, cap - 1)

    def whole(g, at, u):
        return (0, 0, 0)

    return pl.pallas_call(
        functools.partial(precondition_kernel, rows),
        grid_spec=pltpu.PrefetchScalarGridSpec(
            num_scalar_prefetch=2,
            grid=(width,),
            in_specs=[
                pl.BlockSpec((rows * BS, BS), lambda g, at, u: (0, g)),
                pl.BlockSpec((rows, BS, BS), whole),
                pl.BlockSpec((rows, BS, BS), whole),
                pl.BlockSpec((rows, BS, 128), whole),
                pl.BlockSpec((1, ROWS, BS), lambda g, at, u: (g, 0, 0)),
                pl.BlockSpec((1, ROWS, BS), lambda g, at, u: (at[slot(g)], 0, 0)),
            ],
            out_specs=[
                pl.BlockSpec((rows * BS, BS), lambda g, at, u: (0, g)),
                pl.BlockSpec((1, BS, BS), lambda g, at, u: (slot(g), 0, 0)),
            ],
        ),
        out_shape=[
            jax.ShapeDtypeStruct(grad.shape, BF16),
            jax.ShapeDtypeStruct((cap, BS, BS), BF16),
        ],
        compiler_params=pltpu.CompilerParams(vmem_limit_bytes=48 * MIB),
        cost_estimate=pl.CostEstimate(
            flops=8 * BS**3 * rows * width, bytes_accessed=44 * MIB, transcendentals=0
        ),
        name="precondition",
    )(place, used, grad, left, turned_left, la, right, blocks)


def shards(acts, out_grads, weight_grad, old_bases, owner_table):
    n, columns = lax.axis_size("dp"), lax.axis_size("owner")
    me = lax.axis_index("dp")
    blocks_a, blocks_g = acts.shape[1] // BS, out_grads.shape[1] // BS
    count = blocks_a + blocks_g
    cap = old_bases.shape[2]
    tokens = acts.shape[0] * n
    left, right = ceil_div(blocks_a, n), ceil_div(blocks_g, n)
    slots = left + right

    owners = owner_table[0, :, 0]
    order = jnp.arange(count, dtype=jnp.int32)
    same = owners[:, None] == owners[None, :]
    ranks = jnp.sum(jnp.where(same & (order[:, None] < order[None, :]), 1, 0), axis=0).astype(jnp.int32)

    def left_index(a):
        return a // left * slots + a % left

    as_int = functools.partial(jnp.array, dtype=jnp.int32)
    places = as_int([left_index(a) for a in range(blocks_a)]
                    + [g // right * slots + left + g % right for g in range(blocks_g)])
    here = places[None, :] == (me * slots + jnp.arange(slots, dtype=jnp.int32))[:, None]
    old_at = jnp.sum(jnp.where(here, (owners * cap + ranks)[None, :], 0), axis=1).astype(jnp.int32)

    old = lax.all_gather(old_bases[0, 0], "dp", axis=0, tiled=True)
    mom = reduce_blocks(n, slots, moments(n, left, right, acts, out_grads))
    fresh = refresh(mom, old, old_at, tokens)
    blocks, rights = spread(n, columns, left, fresh)
    blocks = blocks.reshape(n * slots, ROWS, BS)

    width = weight_grad.shape[1] // BS
    rights = rights.reshape(n * right, ROWS, BS)
    if n * right != width:
        rights = lax.dynamic_slice_in_dim(rights, me % (n // columns) * width, width, 0)

    left_at = [left_index(a) for a in range(blocks_a)]
    left_basis = jnp.stack([blocks[i, 0:BS] for i in left_at])
    turned_left = jnp.swapaxes(left_basis, 1, 2)
    values = blocks[:, BS]
    la = jnp.stack([values[i] for i in left_at]).astype(F32)
    la = jnp.broadcast_to(la[:, :, None], (blocks_a, BS, 128))

    hit = (owners[None, :] == me) & (ranks[None, :] == jnp.arange(cap, dtype=jnp.int32)[:, None])
    place = jnp.sum(jnp.where(hit, places[None, :], 0), axis=1).astype(jnp.int32)
    used = jnp.any(hit, axis=1)
    chosen = (place[:, None] == jnp.arange(n * slots, dtype=jnp.int32)[None, :]) & used[:, None]
    new_values = jnp.dot(chosen.astype(BF16), values, preferred_element_type=F32).astype(BF16)

    result, new_bases = precondition(
        weight_grad, left_basis, turned_left, la, rights, blocks, place, used.astype(jnp.int32)
    )
    return (result, new_bases[None, None], new_values[None, None])


def solution(mesh):
    placed = (
        P(("groups", "dp"), "owner"),
        P(("groups", "dp"), "owner"),
        P(("groups", "owner"), "dp"),
        P(("groups", "owner"), "dp", None, None, None),
        P("owner", None, None),
    )
    return jax.shard_map(
        shards,
        mesh=mesh,
        in_specs=placed,
        out_specs=(
            P(("groups", "owner"), "dp"),
            P(("groups", "owner"), "dp", None, None, None),
            P(("groups", "owner"), "dp", None, None),
        ),
        check_vma=False,
    )
```

```python
import functools

import jax
import jax.numpy as jnp
from jax import lax
from jax.experimental import pallas as pl
from jax.experimental.pallas import tpu as pltpu
from jax.sharding import PartitionSpec as P

BS = 256
ROWS = BS + 16
ORTHO_STEPS = 8
DAMPING = 0.1
F32 = jnp.float32
BF16 = jnp.bfloat16
MIB = 1 << 20


def dot(a, b, contract):
    return lax.dot_general(a, b, (contract, ((), ())), preferred_element_type=F32)


def ceil_div(a, b):
    return -(-a // b)


def arrange_kernel(each, at, held, *refs):
    out_ref = refs[each]
    for j in range(each):
        old = refs[j][0]
        out_ref[j] = jnp.where(held[pl.program_id(0) * each + j] == 1, old, jnp.zeros_like(old))


def arrange(old, at, held):
    count = at.shape[0]
    each = 8 if count % 8 == 0 else 1

    def one(j):
        return pl.BlockSpec((1, BS, BS), lambda i, at, h: (at[i * each + j], 0, 0))

    return pl.pallas_call(
        functools.partial(arrange_kernel, each),
        grid_spec=pltpu.PrefetchScalarGridSpec(
            num_scalar_prefetch=2,
            grid=(count // each,),
            in_specs=[one(j) for j in range(each)],
            out_specs=pl.BlockSpec((each, BS, BS), lambda i, at, h: (i, 0, 0)),
        ),
        out_shape=jax.ShapeDtypeStruct((count, BS, BS), BF16),
        compiler_params=pltpu.CompilerParams(vmem_limit_bytes=16 * MIB),
        cost_estimate=pl.CostEstimate(flops=0, bytes_accessed=8 * MIB, transcendentals=0),
        name="arrange",
    )(at, held, *([old] * each))


def reduce_kernel(
    n, left, right, acts, grads, old, mom_out, old_out, mom, near, far, own, near_send, near_recv, far_send, far_recv,
):
    slots = left + right
    last_a = acts.shape[1] // (left * BS) - 1
    last_g = grads.shape[1] // (right * BS) - 1
    me = lax.axis_index("dp")
    pairs = n // 2
    chip, core = me // 2, lax.rem(me, 2)
    partner = chip * 2 + (1 - core)

    barrier = pltpu.get_barrier_semaphore()
    pl.semaphore_signal(barrier, inc=1, device_id={"dp": partner})
    for k in range(1, pairs):
        there = lax.rem(chip + k, pairs) * 2 + core
        pl.semaphore_signal(barrier, inc=1, device_id={"dp": there})
    pl.semaphore_wait(barrier, pairs)

    def to_partner(k, part):
        target = lax.rem(chip + k, pairs) * 2 + (1 - core)
        return pltpu.make_async_remote_copy(
            src_ref=(old, mom)[part].at[target],
            dst_ref=near.at[k - 1, part],
            send_sem=near_send.at[k - 1, part],
            recv_sem=near_recv.at[k - 1, part],
            device_id={"dp": partner},
        )

    def to_chip(k, part):
        return pltpu.make_async_remote_copy(
            src_ref=own.at[k - 1, part],
            dst_ref=far.at[k - 1, part],
            send_sem=far_send.at[k - 1, part],
            recv_sem=far_recv.at[k - 1, part],
            device_id={"dp": lax.rem(chip + k, pairs) * 2 + core},
        )

    def moments():
        @pl.loop(0, n)
        def _(r):
            for s in range(slots):
                if s < left:
                    ref, at = acts, (jnp.minimum(r, last_a) * left + s) * BS
                else:
                    ref, at = grads, (jnp.minimum(r, last_g) * right + s - left) * BS
                x = ref[:, pl.ds(pl.multiple_of(at, BS), BS)]
                mom[r, s] = dot(x, x, ((0,), (0,))).astype(BF16)

    def add_near(part):
        for k in range(1, pairs + 1):
            to_partner(k, part).wait()
            mine = lax.rem(chip + k, pairs) * 2 + core

            @pl.loop(0, slots)
            def _(s):
                own[k - 1, part, s] = (
                    (old, mom)[part][mine, s].astype(F32) + near[k - 1, part, s].astype(F32)
                ).astype(BF16)

            if k < pairs:
                to_chip(k, part).start()

    for k in range(1, pairs + 1):
        to_partner(k, 0).start()
    add_near(0)
    moments()
    for k in range(1, pairs + 1):
        to_partner(k, 1).start()
    add_near(1)
    for part in (0, 1):
        for k in range(1, pairs):
            to_chip(k, part).wait()

        @pl.loop(0, slots)
        def _(s):
            total = own[pairs - 1, part, s].astype(F32)
            for k in range(1, pairs):
                total = total + far[k - 1, part, s].astype(F32)
            if part == 0:
                old_out[s] = total.astype(BF16)
            else:
                mom_out[s] = total


def reduce_blocks(n, left, right, acts, grads, old):
    slots = left + right
    pairs = n // 2
    vmem = pl.BlockSpec(memory_space=pltpu.VMEM)
    buffer = pltpu.VMEM((pairs, 2, slots, BS, BS), BF16)
    return pl.pallas_call(
        functools.partial(reduce_kernel, n, left, right),
        out_shape=[
            jax.ShapeDtypeStruct((slots, BS, BS), F32),
            jax.ShapeDtypeStruct((slots, BS, BS), BF16),
        ],
        in_specs=[vmem] * 3,
        out_specs=[vmem, vmem],
        scratch_shapes=[pltpu.VMEM((n, slots, BS, BS), BF16)]
        + [buffer] * 3
        + [pltpu.SemaphoreType.DMA((pairs, 2))] * 4,
        compiler_params=pltpu.CompilerParams(
            collective_id=0, has_side_effects=True, vmem_limit_bytes=56 * MIB
        ),
        cost_estimate=pl.CostEstimate(flops=4096 * MIB, bytes_accessed=16 * MIB, transcendentals=0),
        name="reduce_blocks",
    )(acts, grads, old)


def refresh_kernel(group, tokens, mom_ref, old_ref, out_ref, current):
    for s in range(group):
        moment = mom_ref[s] * (1.0 / tokens)
        product = dot(moment.astype(BF16), old_ref[s], ((1,), (0,)))
        current[s] = product / jnp.sqrt(jnp.sum(product * product) + 1e-06)

    @pl.loop(0, ORTHO_STEPS)
    def _(step):
        rounded = [current[s].astype(BF16) for s in range(group)]
        grams = [dot(y, y, ((0,), (0,))).astype(BF16) for y in rounded]
        for s in range(group):
            current[s] = 1.5 * current[s] - 0.5 * dot(rounded[s], grams[s], ((1,), (0,)))

    for s in range(group):
        moment = mom_ref[s] * (1.0 / tokens)
        high = moment.astype(BF16)
        low = (moment - high.astype(F32)).astype(BF16)
        y = current[s]
        basis = y.astype(BF16)
        applied = dot(high, basis, ((1,), (0,))) + dot(low, basis, ((1,), (0,)))
        top = jnp.mean(applied * y, axis=0, keepdims=True)
        value = top / (jnp.mean(y * y, axis=0, keepdims=True) + 1e-06)
        out_ref[s, 0:BS] = basis
        out_ref[s, BS:ROWS] = jnp.broadcast_to(value, (ROWS - BS, BS)).astype(BF16)


def refresh(mom, old, tokens):
    slots = mom.shape[0]
    group = 4 if slots % 4 == 0 else (2 if slots % 2 == 0 else 1)
    block = pl.BlockSpec((group, BS, BS), lambda i: (i, 0, 0))
    return pl.pallas_call(
        functools.partial(refresh_kernel, group, tokens),
        grid=(slots // group,),
        in_specs=[block, block],
        out_specs=pl.BlockSpec((group, ROWS, BS), lambda i: (i, 0, 0)),
        out_shape=jax.ShapeDtypeStruct((slots, ROWS, BS), BF16),
        scratch_shapes=[pltpu.VMEM((group, BS, BS), F32)],
        compiler_params=pltpu.CompilerParams(vmem_limit_bytes=32 * MIB),
        cost_estimate=pl.CostEstimate(
            flops=36 * slots * BS**3, bytes_accessed=8 * MIB, transcendentals=0
        ),
        name="refresh",
    )(mom, old)


def spread_kernel(
    n, columns, left, cuts, fresh, column_blocks, right, held, up_send, up_recv, down_send, down_recv,
    give_send, give_recv, chip_send, chip_recv, core_send, core_recv, local_sem,
):
    me, here = lax.axis_index("dp"), lax.axis_index("owner")
    per = n // columns
    above = jnp.minimum(here + 1, columns - 1)
    below = jnp.maximum(here - 1, 0)
    has_above, has_below = here < columns - 1, here > 0

    barrier = pltpu.get_barrier_semaphore()
    for k in range(1, n):
        pl.semaphore_signal(barrier, inc=1, device_id={"dp": lax.rem(me + k, n)})

    @pl.when(has_above)
    def _():
        pl.semaphore_signal(barrier, inc=1, device_id={"owner": above})

    @pl.when(has_below)
    def _():
        pl.semaphore_signal(barrier, inc=1, device_id={"owner": below})

    pl.semaphore_wait(barrier, n - 1 + jnp.where(has_above, 1, 0) + jnp.where(has_below, 1, 0))

    held[here] = fresh[left:]

    def along(k, column, piece, send, recv, there):
        return pltpu.make_async_remote_copy(
            src_ref=held.at[column, cuts[piece]],
            dst_ref=held.at[column, cuts[piece]],
            send_sem=send.at[k, piece],
            recv_sem=recv.at[k, piece],
            device_id={"owner": there},
        )

    def clamp(column):
        return jnp.clip(column, 0, columns - 1)

    def up(k, column, piece):
        return along(k, clamp(column), piece, up_send, up_recv, above)

    def down(k, column, piece):
        return along(k, clamp(column), piece, down_send, down_recv, below)

    def give(column, target, piece):
        return pltpu.make_async_remote_copy(
            src_ref=held.at[column, cuts[piece]],
            dst_ref=right.at[me, cuts[piece]],
            send_sem=give_send.at[target, piece],
            recv_sem=give_recv.at[me, piece],
            device_id={"dp": target},
        )

    def taken(source, piece):
        return pltpu.make_async_remote_copy(
            src_ref=held.at[0, cuts[piece]],
            dst_ref=right.at[source, cuts[piece]],
            send_sem=give_send.at[source, piece],
            recv_sem=give_recv.at[source, piece],
            device_id={"dp": source},
        )

    def keep(column, piece):
        return pltpu.make_async_copy(
            held.at[column, cuts[piece]], right.at[me, cuts[piece]], local_sem.at[piece]
        )

    def share(column, piece):
        for h in range(per):
            target = column * per + h

            @pl.when(target != me)
            def _():
                give(column, target, piece).start()

            @pl.when(target == me)
            def _():
                keep(column, piece).start()

    pairs = n // 2
    chip, core = me // 2, lax.rem(me, 2)
    partner = chip * 2 + (1 - core)

    def to_chip(k):
        return pltpu.make_async_remote_copy(
            src_ref=fresh,
            dst_ref=column_blocks.at[me],
            send_sem=chip_send.at[k - 1],
            recv_sem=chip_recv.at[k - 1],
            device_id={"dp": lax.rem(chip + k, pairs) * 2 + core},
        )

    def source(k):
        return lax.rem(chip + pairs - k, pairs) * 2 + core

    def to_partner(k):
        return pltpu.make_async_remote_copy(
            src_ref=fresh if k == 0 else column_blocks.at[source(k)],
            dst_ref=column_blocks.at[source(k)],
            send_sem=core_send.at[k],
            recv_sem=core_recv.at[k],
            device_id={"dp": partner},
        )

    mine = pltpu.make_async_copy(fresh, column_blocks.at[me], local_sem.at[len(cuts)])
    for piece in range(len(cuts)):

        @pl.when(has_above)
        def _():
            up(0, here, piece).start()

        @pl.when(has_below)
        def _():
            down(0, here, piece).start()

    for piece in range(len(cuts)):
        share(here, piece)
    mine.start()
    for j in range(1, pairs):
        to_chip(j).start()
    to_partner(0).start()

    for k in range(columns - 1):
        if k == 1:
            for j in range(1, pairs):
                to_chip(j).wait_recv()
                to_partner(j).start()
        for piece in range(len(cuts)):

            @pl.when(here - 1 - k >= 0)
            def _():
                up(k, here - 1 - k, piece).wait_recv()
                if k + 1 < columns - 1:

                    @pl.when(has_above)
                    def _():
                        up(k + 1, here - 1 - k, piece).start()

                share(clamp(here - 1 - k), piece)

            @pl.when(here + 1 + k <= columns - 1)
            def _():
                down(k, here + 1 + k, piece).wait_recv()
                if k + 1 < columns - 1:

                    @pl.when(has_below)
                    def _():
                        down(k + 1, here + 1 + k, piece).start()

                share(clamp(here + 1 + k), piece)

    for k in range(columns - 1):
        for piece in range(len(cuts)):

            @pl.when(has_above & (here - k >= 0))
            def _():
                up(k, here - k, piece).wait_send()

            @pl.when(has_below & (here + k <= columns - 1))
            def _():
                down(k, here + k, piece).wait_send()

    mine.wait()
    for k in range(pairs):
        to_partner(k).wait()
        if k > 0:
            to_chip(k).wait_send()
    for piece in range(len(cuts)):
        keep(here, piece).wait()
        for k in range(1, n):
            other = lax.rem(me + k, n)
            taken(other, piece).wait_send()
            taken(other, piece).wait_recv()


def spread(n, columns, left, fresh):
    slots = fresh.shape[0]
    dma = pltpu.SemaphoreType.DMA
    some = slots - left
    pieces = 3 if some % 3 == 0 else 1
    cuts = [pl.ds(i * (some // pieces), some // pieces) for i in range(pieces)]
    vmem = pl.BlockSpec(memory_space=pltpu.VMEM)
    return pl.pallas_call(
        functools.partial(spread_kernel, n, columns, left, cuts),
        out_shape=[
            jax.ShapeDtypeStruct((n, slots, ROWS, BS), BF16),
            jax.ShapeDtypeStruct((n, slots - left, ROWS, BS), BF16),
        ],
        in_specs=[vmem],
        out_specs=[vmem, vmem],
        scratch_shapes=[pltpu.VMEM((columns, slots - left, ROWS, BS), BF16)]
        + [dma((columns - 1, pieces))] * 4
        + [dma((n, pieces))] * 2
        + [dma((max(1, n // 2 - 1),))] * 2
        + [dma((n // 2,))] * 2
        + [dma((pieces + 1,))],
        compiler_params=pltpu.CompilerParams(
            collective_id=1, has_side_effects=True, vmem_limit_bytes=56 * MIB
        ),
        cost_estimate=pl.CostEstimate(flops=0, bytes_accessed=16 * MIB, transcendentals=0),
        name="spread",
    )(fresh)


def precondition_kernel(
    rows, place, used, grad_ref, left_ref, turned_left_ref, la_ref, right_ref, block_ref, out_ref, bases_ref,
):
    slot = jnp.minimum(pl.program_id(0), used.shape[0] - 1)
    basis = right_ref[0, 0:BS]
    lg = right_ref[0, BS:ROWS].astype(F32)[0:1]
    turned = [
        dot(turned_left_ref[a], grad_ref[a * BS : (a + 1) * BS], ((1,), (0,))).astype(BF16)
        for a in range(rows)
    ]
    rotated = [dot(turned[a], basis, ((1,), (0,))) for a in range(rows)]
    scaled = [
        (rotated[a] / (la_ref[a][:, 0:1] * lg + DAMPING)).astype(BF16) for a in range(rows)
    ]
    returned = [dot(scaled[a], basis, ((1,), (1,))).astype(BF16) for a in range(rows)]
    for a in range(rows):
        out_ref[a * BS : (a + 1) * BS] = dot(left_ref[a], returned[a], ((1,), (0,))).astype(BF16)
    block = block_ref[0, 0:BS]
    bases_ref[0] = jnp.where(used[slot] == 1, block, jnp.zeros_like(block))


def precondition(grad, left, turned_left, la, right, blocks, place, used):
    rows, width = grad.shape[0] // BS, grad.shape[1] // BS
    cap = place.shape[0]
    assert width >= cap

    def slot(g):
        return jnp.minimum(g, cap - 1)

    def whole(g, at, u):
        return (0, 0, 0)

    return pl.pallas_call(
        functools.partial(precondition_kernel, rows),
        grid_spec=pltpu.PrefetchScalarGridSpec(
            num_scalar_prefetch=2,
            grid=(width,),
            in_specs=[
                pl.BlockSpec((rows * BS, BS), lambda g, at, u: (0, g)),
                pl.BlockSpec((rows, BS, BS), whole),
                pl.BlockSpec((rows, BS, BS), whole),
                pl.BlockSpec((rows, BS, 128), whole),
                pl.BlockSpec((1, ROWS, BS), lambda g, at, u: (g, 0, 0)),
                pl.BlockSpec((1, ROWS, BS), lambda g, at, u: (at[slot(g)], 0, 0)),
            ],
            out_specs=[
                pl.BlockSpec((rows * BS, BS), lambda g, at, u: (0, g)),
                pl.BlockSpec((1, BS, BS), lambda g, at, u: (slot(g), 0, 0)),
            ],
        ),
        out_shape=[
            jax.ShapeDtypeStruct(grad.shape, BF16),
            jax.ShapeDtypeStruct((cap, BS, BS), BF16),
        ],
        compiler_params=pltpu.CompilerParams(vmem_limit_bytes=48 * MIB),
        cost_estimate=pl.CostEstimate(
            flops=8 * BS**3 * rows * width, bytes_accessed=44 * MIB, transcendentals=0
        ),
        name="precondition",
    )(place, used, grad, left, turned_left, la, right, blocks)


def shards(acts, out_grads, weight_grad, old_bases, owner_table):
    n, columns = lax.axis_size("dp"), lax.axis_size("owner")
    me = lax.axis_index("dp")
    blocks_a, blocks_g = acts.shape[1] // BS, out_grads.shape[1] // BS
    count = blocks_a + blocks_g
    cap = old_bases.shape[2]
    tokens = acts.shape[0] * n
    left, right = ceil_div(blocks_a, n), ceil_div(blocks_g, n)
    slots = left + right

    owners = owner_table[0, :, 0]
    order = jnp.arange(count, dtype=jnp.int32)
    same = owners[:, None] == owners[None, :]
    ranks = jnp.sum(jnp.where(same & (order[:, None] < order[None, :]), 1, 0), axis=0).astype(jnp.int32)

    def left_index(a):
        return a // left * slots + a % left

    as_int = functools.partial(jnp.array, dtype=jnp.int32)
    places = as_int([left_index(a) for a in range(blocks_a)]
                    + [g // right * slots + left + g % right for g in range(blocks_g)])
    hit_at = places[None, :] == jnp.arange(n * slots, dtype=jnp.int32)[:, None]
    hit_at = hit_at & (owners == me)[None, :]
    old_at = jnp.sum(jnp.where(hit_at, ranks[None, :], 0), axis=1).astype(jnp.int32)
    held = jnp.sum(jnp.where(hit_at, 1, 0), axis=1).astype(jnp.int32)

    old = arrange(old_bases[0, 0], old_at, held).reshape(n, slots, BS, BS)
    mom, old = reduce_blocks(n, left, right, acts, out_grads, old)
    fresh = refresh(mom, old, tokens)
    blocks, rights = spread(n, columns, left, fresh)
    blocks = blocks.reshape(n * slots, ROWS, BS)

    width = weight_grad.shape[1] // BS
    rights = rights.reshape(n * right, ROWS, BS)
    if n * right != width:
        rights = lax.dynamic_slice_in_dim(rights, me % (n // columns) * width, width, 0)

    left_at = [left_index(a) for a in range(blocks_a)]
    left_basis = jnp.stack([blocks[i, 0:BS] for i in left_at])
    turned_left = jnp.swapaxes(left_basis, 1, 2)
    values = blocks[:, BS]
    la = jnp.stack([values[i] for i in left_at]).astype(F32)
    la = jnp.broadcast_to(la[:, :, None], (blocks_a, BS, 128))

    hit = (owners[None, :] == me) & (ranks[None, :] == jnp.arange(cap, dtype=jnp.int32)[:, None])
    place = jnp.sum(jnp.where(hit, places[None, :], 0), axis=1).astype(jnp.int32)
    used = jnp.any(hit, axis=1)
    chosen = (place[:, None] == jnp.arange(n * slots, dtype=jnp.int32)[None, :]) & used[:, None]
    new_values = jnp.dot(chosen.astype(BF16), values, preferred_element_type=F32).astype(BF16)

    result, new_bases = precondition(
        weight_grad, left_basis, turned_left, la, rights, blocks, place, used.astype(jnp.int32)
    )
    return (result, new_bases[None, None], new_values[None, None])


def solution(mesh):
    placed = (
        P(("groups", "dp"), "owner"),
        P(("groups", "dp"), "owner"),
        P(("groups", "owner"), "dp"),
        P(("groups", "owner"), "dp", None, None, None),
        P("owner", None, None),
    )
    return jax.shard_map(
        shards,
        mesh=mesh,
        in_specs=placed,
        out_specs=(
            P(("groups", "owner"), "dp"),
            P(("groups", "owner"), "dp", None, None, None),
            P(("groups", "owner"), "dp", None, None),
        ),
        check_vma=False,
    )
```

```python
import functools

import jax
import jax.numpy as jnp
from jax import lax
from jax.experimental import pallas as pl
from jax.experimental.pallas import tpu as pltpu
from jax.sharding import PartitionSpec as P

BS = 256
ROWS = BS + 16
ORTHO_STEPS = 8
DAMPING = 0.1
F32 = jnp.float32
BF16 = jnp.bfloat16
MIB = 1 << 20


def dot(a, b, contract):
    return lax.dot_general(a, b, (contract, ((), ())), preferred_element_type=F32)


def ceil_div(a, b):
    return -(-a // b)


def arrange_kernel(each, at, held, *refs):
    out_ref = refs[each]
    for j in range(each):
        old = refs[j][0]
        out_ref[j] = jnp.where(held[pl.program_id(0) * each + j] == 1, old, jnp.zeros_like(old))


def arrange(old, at, held):
    count = at.shape[0]
    each = 8 if count % 8 == 0 else 1

    def one(j):
        return pl.BlockSpec((1, BS, BS), lambda i, at, h: (at[i * each + j], 0, 0))

    return pl.pallas_call(
        functools.partial(arrange_kernel, each),
        grid_spec=pltpu.PrefetchScalarGridSpec(
            num_scalar_prefetch=2,
            grid=(count // each,),
            in_specs=[one(j) for j in range(each)],
            out_specs=pl.BlockSpec((each, BS, BS), lambda i, at, h: (i, 0, 0)),
        ),
        out_shape=jax.ShapeDtypeStruct((count, BS, BS), BF16),
        compiler_params=pltpu.CompilerParams(vmem_limit_bytes=16 * MIB),
        cost_estimate=pl.CostEstimate(flops=0, bytes_accessed=8 * MIB, transcendentals=0),
        name="arrange",
    )(at, held, *([old] * each))


def reduce_kernel(
    n, left, right, acts, grads, old, mom_out, old_out, mom, near, far, own, near_send, near_recv, far_send, far_recv,
):
    slots = left + right
    last_a = acts.shape[1] // (left * BS) - 1
    last_g = grads.shape[1] // (right * BS) - 1
    me = lax.axis_index("dp")
    pairs = n // 2
    chip, core = me // 2, lax.rem(me, 2)
    partner = chip * 2 + (1 - core)

    barrier = pltpu.get_barrier_semaphore()
    pl.semaphore_signal(barrier, inc=1, device_id={"dp": partner})
    for k in range(1, pairs):
        there = lax.rem(chip + k, pairs) * 2 + core
        pl.semaphore_signal(barrier, inc=1, device_id={"dp": there})
    pl.semaphore_wait(barrier, pairs)

    def to_partner(k, part):
        target = lax.rem(chip + k, pairs) * 2 + (1 - core)
        return pltpu.make_async_remote_copy(
            src_ref=(old, mom)[part].at[target],
            dst_ref=near.at[k - 1, part],
            send_sem=near_send.at[k - 1, part],
            recv_sem=near_recv.at[k - 1, part],
            device_id={"dp": partner},
        )

    def to_chip(k, part):
        return pltpu.make_async_remote_copy(
            src_ref=own.at[k - 1, part],
            dst_ref=far.at[k - 1, part],
            send_sem=far_send.at[k - 1, part],
            recv_sem=far_recv.at[k - 1, part],
            device_id={"dp": lax.rem(chip + k, pairs) * 2 + core},
        )

    def moments():
        @pl.loop(0, n)
        def _(r):
            for s in range(slots):
                if s < left:
                    ref, at = acts, (jnp.minimum(r, last_a) * left + s) * BS
                else:
                    ref, at = grads, (jnp.minimum(r, last_g) * right + s - left) * BS
                x = ref[:, pl.ds(pl.multiple_of(at, BS), BS)]
                mom[r, s] = dot(x, x, ((0,), (0,))).astype(BF16)

    def add_near(part):
        for k in range(1, pairs + 1):
            to_partner(k, part).wait()
            mine = lax.rem(chip + k, pairs) * 2 + core

            @pl.loop(0, slots)
            def _(s):
                own[k - 1, part, s] = (
                    (old, mom)[part][mine, s].astype(F32) + near[k - 1, part, s].astype(F32)
                ).astype(BF16)

            if k < pairs:
                to_chip(k, part).start()

    for k in range(1, pairs + 1):
        to_partner(k, 0).start()
    add_near(0)
    moments()
    for k in range(1, pairs + 1):
        to_partner(k, 1).start()
    add_near(1)
    for part in (0, 1):
        for k in range(1, pairs):
            to_chip(k, part).wait()

        @pl.loop(0, slots)
        def _(s):
            total = own[pairs - 1, part, s].astype(F32)
            for k in range(1, pairs):
                total = total + far[k - 1, part, s].astype(F32)
            if part == 0:
                old_out[s] = total.astype(BF16)
            else:
                mom_out[s] = total


def reduce_blocks(n, left, right, acts, grads, old):
    slots = left + right
    pairs = n // 2
    vmem = pl.BlockSpec(memory_space=pltpu.VMEM)
    buffer = pltpu.VMEM((pairs, 2, slots, BS, BS), BF16)
    return pl.pallas_call(
        functools.partial(reduce_kernel, n, left, right),
        out_shape=[
            jax.ShapeDtypeStruct((slots, BS, BS), F32),
            jax.ShapeDtypeStruct((slots, BS, BS), BF16),
        ],
        in_specs=[vmem] * 3,
        out_specs=[vmem, vmem],
        scratch_shapes=[pltpu.VMEM((n, slots, BS, BS), BF16)]
        + [buffer] * 3
        + [pltpu.SemaphoreType.DMA((pairs, 2))] * 4,
        compiler_params=pltpu.CompilerParams(
            collective_id=0, has_side_effects=True, vmem_limit_bytes=56 * MIB
        ),
        cost_estimate=pl.CostEstimate(flops=4096 * MIB, bytes_accessed=16 * MIB, transcendentals=0),
        name="reduce_blocks",
    )(acts, grads, old)


def refresh_kernel(group, tokens, mom_ref, old_ref, out_ref, current):
    for s in range(group):
        moment = mom_ref[s] * (1.0 / tokens)
        product = dot(moment.astype(BF16), old_ref[s], ((1,), (0,)))
        current[s] = product / jnp.sqrt(jnp.sum(product * product) + 1e-06)

    @pl.loop(0, ORTHO_STEPS)
    def _(step):
        rounded = [current[s].astype(BF16) for s in range(group)]
        grams = [dot(y, y, ((0,), (0,))).astype(BF16) for y in rounded]
        for s in range(group):
            current[s] = 1.5 * current[s] - 0.5 * dot(rounded[s], grams[s], ((1,), (0,)))

    for s in range(group):
        moment = mom_ref[s] * (1.0 / tokens)
        high = moment.astype(BF16)
        low = (moment - high.astype(F32)).astype(BF16)
        y = current[s]
        basis = y.astype(BF16)
        applied = dot(high, basis, ((1,), (0,))) + dot(low, basis, ((1,), (0,)))
        top = jnp.mean(applied * y, axis=0, keepdims=True)
        value = top / (jnp.mean(y * y, axis=0, keepdims=True) + 1e-06)
        out_ref[s, 0:BS] = basis
        out_ref[s, BS:ROWS] = jnp.broadcast_to(value, (ROWS - BS, BS)).astype(BF16)


def refresh(mom, old, tokens):
    slots = mom.shape[0]
    group = 8 if slots % 8 == 0 else (2 if slots % 2 == 0 else 1)
    block = pl.BlockSpec((group, BS, BS), lambda i: (i, 0, 0))
    return pl.pallas_call(
        functools.partial(refresh_kernel, group, tokens),
        grid=(slots // group,),
        in_specs=[block, block],
        out_specs=pl.BlockSpec((group, ROWS, BS), lambda i: (i, 0, 0)),
        out_shape=jax.ShapeDtypeStruct((slots, ROWS, BS), BF16),
        scratch_shapes=[pltpu.VMEM((group, BS, BS), F32)],
        compiler_params=pltpu.CompilerParams(vmem_limit_bytes=32 * MIB),
        cost_estimate=pl.CostEstimate(
            flops=36 * slots * BS**3, bytes_accessed=8 * MIB, transcendentals=0
        ),
        name="refresh",
    )(mom, old)


def spread_kernel(
    n, columns, left, cuts, fresh, column_blocks, right, held, up_send, up_recv, down_send, down_recv,
    give_send, give_recv, chip_send, chip_recv, core_send, core_recv, local_sem,
):
    me, here = lax.axis_index("dp"), lax.axis_index("owner")
    per = n // columns
    above = jnp.minimum(here + 1, columns - 1)
    below = jnp.maximum(here - 1, 0)
    has_above, has_below = here < columns - 1, here > 0

    barrier = pltpu.get_barrier_semaphore()
    for k in range(1, n):
        pl.semaphore_signal(barrier, inc=1, device_id={"dp": lax.rem(me + k, n)})

    @pl.when(has_above)
    def _():
        pl.semaphore_signal(barrier, inc=1, device_id={"owner": above})

    @pl.when(has_below)
    def _():
        pl.semaphore_signal(barrier, inc=1, device_id={"owner": below})

    pl.semaphore_wait(barrier, n - 1 + jnp.where(has_above, 1, 0) + jnp.where(has_below, 1, 0))

    held[here] = fresh[left:]

    def along(k, column, piece, send, recv, there):
        return pltpu.make_async_remote_copy(
            src_ref=held.at[column, cuts[piece]],
            dst_ref=held.at[column, cuts[piece]],
            send_sem=send.at[k, piece],
            recv_sem=recv.at[k, piece],
            device_id={"owner": there},
        )

    def clamp(column):
        return jnp.clip(column, 0, columns - 1)

    def up(k, column, piece):
        return along(k, clamp(column), piece, up_send, up_recv, above)

    def down(k, column, piece):
        return along(k, clamp(column), piece, down_send, down_recv, below)

    def give(column, target, piece):
        return pltpu.make_async_remote_copy(
            src_ref=held.at[column, cuts[piece]],
            dst_ref=right.at[me, cuts[piece]],
            send_sem=give_send.at[target, piece],
            recv_sem=give_recv.at[me, piece],
            device_id={"dp": target},
        )

    def taken(source, piece):
        return pltpu.make_async_remote_copy(
            src_ref=held.at[0, cuts[piece]],
            dst_ref=right.at[source, cuts[piece]],
            send_sem=give_send.at[source, piece],
            recv_sem=give_recv.at[source, piece],
            device_id={"dp": source},
        )

    def keep(column, piece):
        return pltpu.make_async_copy(
            held.at[column, cuts[piece]], right.at[me, cuts[piece]], local_sem.at[piece]
        )

    def share(column, piece):
        for h in range(per):
            target = column * per + h

            @pl.when(target != me)
            def _():
                give(column, target, piece).start()

            @pl.when(target == me)
            def _():
                keep(column, piece).start()

    pairs = n // 2
    chip, core = me // 2, lax.rem(me, 2)
    partner = chip * 2 + (1 - core)

    def to_chip(k):
        return pltpu.make_async_remote_copy(
            src_ref=fresh,
            dst_ref=column_blocks.at[me],
            send_sem=chip_send.at[k - 1],
            recv_sem=chip_recv.at[k - 1],
            device_id={"dp": lax.rem(chip + k, pairs) * 2 + core},
        )

    def source(k):
        return lax.rem(chip + pairs - k, pairs) * 2 + core

    def to_partner(k):
        return pltpu.make_async_remote_copy(
            src_ref=fresh if k == 0 else column_blocks.at[source(k)],
            dst_ref=column_blocks.at[source(k)],
            send_sem=core_send.at[k],
            recv_sem=core_recv.at[k],
            device_id={"dp": partner},
        )

    mine = pltpu.make_async_copy(fresh, column_blocks.at[me], local_sem.at[len(cuts)])
    for piece in range(len(cuts)):

        @pl.when(has_above)
        def _():
            up(0, here, piece).start()

        @pl.when(has_below)
        def _():
            down(0, here, piece).start()

    for piece in range(len(cuts)):
        share(here, piece)
    mine.start()
    for j in range(1, pairs):
        to_chip(j).start()
    to_partner(0).start()

    for k in range(columns - 1):
        if k == 1:
            for j in range(1, pairs):
                to_chip(j).wait_recv()
                to_partner(j).start()
        for piece in range(len(cuts)):

            @pl.when(here - 1 - k >= 0)
            def _():
                up(k, here - 1 - k, piece).wait_recv()
                if k + 1 < columns - 1:

                    @pl.when(has_above)
                    def _():
                        up(k + 1, here - 1 - k, piece).start()

                share(clamp(here - 1 - k), piece)

            @pl.when(here + 1 + k <= columns - 1)
            def _():
                down(k, here + 1 + k, piece).wait_recv()
                if k + 1 < columns - 1:

                    @pl.when(has_below)
                    def _():
                        down(k + 1, here + 1 + k, piece).start()

                share(clamp(here + 1 + k), piece)

    for k in range(columns - 1):
        for piece in range(len(cuts)):

            @pl.when(has_above & (here - k >= 0))
            def _():
                up(k, here - k, piece).wait_send()

            @pl.when(has_below & (here + k <= columns - 1))
            def _():
                down(k, here + k, piece).wait_send()

    mine.wait()
    for k in range(pairs):
        to_partner(k).wait()
        if k > 0:
            to_chip(k).wait_send()
    for piece in range(len(cuts)):
        keep(here, piece).wait()
        for k in range(1, n):
            other = lax.rem(me + k, n)
            taken(other, piece).wait_send()
            taken(other, piece).wait_recv()


def spread(n, columns, left, fresh):
    slots = fresh.shape[0]
    dma = pltpu.SemaphoreType.DMA
    some = slots - left
    pieces = 3 if some % 3 == 0 else 1
    cuts = [pl.ds(i * (some // pieces), some // pieces) for i in range(pieces)]
    vmem = pl.BlockSpec(memory_space=pltpu.VMEM)
    return pl.pallas_call(
        functools.partial(spread_kernel, n, columns, left, cuts),
        out_shape=[
            jax.ShapeDtypeStruct((n, slots, ROWS, BS), BF16),
            jax.ShapeDtypeStruct((n, slots - left, ROWS, BS), BF16),
        ],
        in_specs=[vmem],
        out_specs=[vmem, vmem],
        scratch_shapes=[pltpu.VMEM((columns, slots - left, ROWS, BS), BF16)]
        + [dma((columns - 1, pieces))] * 4
        + [dma((n, pieces))] * 2
        + [dma((max(1, n // 2 - 1),))] * 2
        + [dma((n // 2,))] * 2
        + [dma((pieces + 1,))],
        compiler_params=pltpu.CompilerParams(
            collective_id=1, has_side_effects=True, vmem_limit_bytes=56 * MIB
        ),
        cost_estimate=pl.CostEstimate(flops=0, bytes_accessed=16 * MIB, transcendentals=0),
        name="spread",
    )(fresh)


def precondition_kernel(
    rows, place, used, grad_ref, left_ref, turned_left_ref, la_ref, right_ref, block_ref, out_ref, bases_ref,
):
    slot = jnp.minimum(pl.program_id(0), used.shape[0] - 1)
    basis = right_ref[0, 0:BS]
    lg = right_ref[0, BS:ROWS].astype(F32)[0:1]
    turned = [
        dot(turned_left_ref[a], grad_ref[a * BS : (a + 1) * BS], ((1,), (0,))).astype(BF16)
        for a in range(rows)
    ]
    rotated = [dot(turned[a], basis, ((1,), (0,))) for a in range(rows)]
    scaled = []
    for a in range(rows):
        divisor = la_ref[a][:, 0:1] * lg + DAMPING
        inverse = pl.reciprocal(divisor, approx=True)
        inverse = inverse * (2.0 - divisor * inverse)
        scaled.append((rotated[a] * inverse).astype(BF16))
    returned = [dot(scaled[a], basis, ((1,), (1,))).astype(BF16) for a in range(rows)]
    for a in range(rows):
        out_ref[a * BS : (a + 1) * BS] = dot(left_ref[a], returned[a], ((1,), (0,))).astype(BF16)
    block = block_ref[0, 0:BS]
    bases_ref[0] = jnp.where(used[slot] == 1, block, jnp.zeros_like(block))


def precondition(grad, left, turned_left, la, right, blocks, place, used):
    rows, width = grad.shape[0] // BS, grad.shape[1] // BS
    cap = place.shape[0]
    assert width >= cap

    def slot(g):
        return jnp.minimum(g, cap - 1)

    def whole(g, at, u):
        return (0, 0, 0)

    return pl.pallas_call(
        functools.partial(precondition_kernel, rows),
        grid_spec=pltpu.PrefetchScalarGridSpec(
            num_scalar_prefetch=2,
            grid=(width,),
            in_specs=[
                pl.BlockSpec((rows * BS, BS), lambda g, at, u: (0, g)),
                pl.BlockSpec((rows, BS, BS), whole),
                pl.BlockSpec((rows, BS, BS), whole),
                pl.BlockSpec((rows, BS, 128), whole),
                pl.BlockSpec((1, ROWS, BS), lambda g, at, u: (g, 0, 0)),
                pl.BlockSpec((1, ROWS, BS), lambda g, at, u: (at[slot(g)], 0, 0)),
            ],
            out_specs=[
                pl.BlockSpec((rows * BS, BS), lambda g, at, u: (0, g)),
                pl.BlockSpec((1, BS, BS), lambda g, at, u: (slot(g), 0, 0)),
            ],
        ),
        out_shape=[
            jax.ShapeDtypeStruct(grad.shape, BF16),
            jax.ShapeDtypeStruct((cap, BS, BS), BF16),
        ],
        compiler_params=pltpu.CompilerParams(vmem_limit_bytes=48 * MIB),
        cost_estimate=pl.CostEstimate(
            flops=8 * BS**3 * rows * width, bytes_accessed=44 * MIB, transcendentals=0
        ),
        name="precondition",
    )(place, used, grad, left, turned_left, la, right, blocks)


def shards(acts, out_grads, weight_grad, old_bases, owner_table):
    n, columns = lax.axis_size("dp"), lax.axis_size("owner")
    me = lax.axis_index("dp")
    blocks_a, blocks_g = acts.shape[1] // BS, out_grads.shape[1] // BS
    count = blocks_a + blocks_g
    cap = old_bases.shape[2]
    tokens = acts.shape[0] * n
    left, right = ceil_div(blocks_a, n), ceil_div(blocks_g, n)
    slots = left + right

    owners = owner_table[0, :, 0]
    order = jnp.arange(count, dtype=jnp.int32)
    same = owners[:, None] == owners[None, :]
    ranks = jnp.sum(jnp.where(same & (order[:, None] < order[None, :]), 1, 0), axis=0).astype(jnp.int32)

    def left_index(a):
        return a // left * slots + a % left

    as_int = functools.partial(jnp.array, dtype=jnp.int32)
    places = as_int([left_index(a) for a in range(blocks_a)]
                    + [g // right * slots + left + g % right for g in range(blocks_g)])
    hit_at = places[None, :] == jnp.arange(n * slots, dtype=jnp.int32)[:, None]
    hit_at = hit_at & (owners == me)[None, :]
    old_at = jnp.sum(jnp.where(hit_at, ranks[None, :], 0), axis=1).astype(jnp.int32)
    held = jnp.sum(jnp.where(hit_at, 1, 0), axis=1).astype(jnp.int32)

    old = arrange(old_bases[0, 0], old_at, held).reshape(n, slots, BS, BS)
    mom, old = reduce_blocks(n, left, right, acts, out_grads, old)
    fresh = refresh(mom, old, tokens)
    blocks, rights = spread(n, columns, left, fresh)
    blocks = blocks.reshape(n * slots, ROWS, BS)

    width = weight_grad.shape[1] // BS
    rights = rights.reshape(n * right, ROWS, BS)
    if n * right != width:
        rights = lax.dynamic_slice_in_dim(rights, me % (n // columns) * width, width, 0)

    left_at = [left_index(a) for a in range(blocks_a)]
    left_basis = jnp.stack([blocks[i, 0:BS] for i in left_at])
    turned_left = jnp.swapaxes(left_basis, 1, 2)
    values = blocks[:, BS]
    la = jnp.stack([values[i] for i in left_at]).astype(F32)
    la = jnp.broadcast_to(la[:, :, None], (blocks_a, BS, 128))

    hit = (owners[None, :] == me) & (ranks[None, :] == jnp.arange(cap, dtype=jnp.int32)[:, None])
    place = jnp.sum(jnp.where(hit, places[None, :], 0), axis=1).astype(jnp.int32)
    used = jnp.any(hit, axis=1)
    chosen = (place[:, None] == jnp.arange(n * slots, dtype=jnp.int32)[None, :]) & used[:, None]
    new_values = jnp.dot(chosen.astype(BF16), values, preferred_element_type=F32).astype(BF16)

    result, new_bases = precondition(
        weight_grad, left_basis, turned_left, la, rights, blocks, place, used.astype(jnp.int32)
    )
    return (result, new_bases[None, None], new_values[None, None])


def solution(mesh):
    placed = (
        P(("groups", "dp"), "owner"),
        P(("groups", "dp"), "owner"),
        P(("groups", "owner"), "dp"),
        P(("groups", "owner"), "dp", None, None, None),
        P("owner", None, None),
    )
    return jax.shard_map(
        shards,
        mesh=mesh,
        in_specs=placed,
        out_specs=(
            P(("groups", "owner"), "dp"),
            P(("groups", "owner"), "dp", None, None, None),
            P(("groups", "owner"), "dp", None, None),
        ),
        check_vma=False,
    )
```
